256 devices in a mesh: occ: 16 (over y, x), aux: 16 (over z, core).
Axes of the slice: x: 4, y: 4, z: 8, core: 2. Of those that a mesh axis runs over, the one named last changes fastest.
Arguments:
- b_factors: bfloat16 [4096, 9216], P('occ', 'aux'), may hold values from -1 to 1, as said below
- occ_energy: float32 [16], P('occ'), may hold values from -1.5 to -0.3
- vir_energy: float32 [256], replicated, may hold values from 0.1 to 2.5
Outputs:
- gamma: float32 [4096, 9216], P('occ', 'aux')
The draws below stay inside these ranges and needn't reach their ends.
Inputs may be any that keep to these rules, and one draw needn't show every extreme that they name: `b_factors`: real entries; rows are independent of one another.
All inputs are finite; a program needn't handle non-finite values.
Results may differ from the reference program's by a relative error of at most 0.0025.
Values may be sent and summed in bfloat16 or wider, within the bound.
No kernel may reach another device: no remote copies, remote signals or barrier semaphores. Data moves between devices by JAX's collectives and lax.ppermute only.
A program may use at most 64 MiB of HBM per device.

```python
import jax
import jax.numpy as jnp

VP = 256
NAUX = 9216
OCC = 16


def draw_b_factors(key, part):
    key = jax.random.fold_in(key, 7)
    factor = (4.0 / (NAUX + (OCC * VP * NAUX) ** 0.5)) ** (1.0 / 3.0)
    first_key = jax.random.fold_in(key, 0)
    values = jnp.clip(jax.random.normal(first_key, (OCC * VP, NAUX), jnp.float32), -3.5, 3.5)
    return (values * factor).astype(jnp.bfloat16)


def block_levels(stream_key, shape, pieces, smallest, top_value):
    loudness, own = 1.0, jax.random.fold_in(stream_key, 6)
    for dim, parts in pieces:
        draws = jnp.exp(jax.random.uniform(jax.random.fold_in(own, dim), (parts,), jnp.float32, smallest / len(pieces), top_value / len(pieces)))
        loudness = loudness * jnp.repeat(draws, shape[dim] // parts).reshape([-1 if axis == dim else 1 for axis in range(len(shape))])
    return loudness


def setup_inputs(seed: int = 0) -> dict:
    key_of = jax.random.split(jax.random.key(seed), 4)
    return {
        "b_factors": draw_b_factors(jax.random.fold_in(key_of[3], 71), 0),
        "occ_energy": jnp.clip(-1.5 + 1.2 * jax.random.uniform(key_of[1], (OCC,), jnp.float32) ** block_levels(key_of[1], (OCC,), ((0, 16),), -0.2, 0.2), -1.5, -0.3),
        "vir_energy": jnp.clip(jax.random.uniform(key_of[2], (VP,), jnp.float32, 0.1, 2.5), 0.1, 2.5),
    }


def reference(b_factors, occ_energy, vir_energy):
    integrals = jnp.dot(b_factors, b_factors.T, preferred_element_type=jnp.float32)
    row_energy = jnp.tile(vir_energy, OCC) - jnp.repeat(occ_energy, VP)
    denominator = row_energy[:, None] + row_energy[None, :]
    amplitude = (integrals / denominator).astype(jnp.bfloat16)
    return jnp.dot(amplitude, b_factors, preferred_element_type=jnp.float32)
```

```python
import functools

import jax
import jax.numpy as jnp
from jax import lax
from jax.experimental import pallas as pl
from jax.experimental.pallas import tpu as pltpu
from jax.sharding import PartitionSpec as P

HELD = (0, 1, 3, 11, 12)
PAIRS = ((0, 0), (0, 1), (0, 2), (0, 4), (0, 3), (1, 2), (1, 3), (2, 4), (2, 3))
ONE_WAY = ((0, 0), (2, 3))
STRIP = 16
VMEM = pl.BlockSpec(memory_space=pltpu.VMEM)
SMEM = pl.BlockSpec(memory_space=pltpu.SMEM)


def rotate(array, axis, by):
    size = lax.axis_size(axis)
    return lax.ppermute(array, axis, [(i, (i + by) % size) for i in range(size)])


def sibling(array):
    return lax.ppermute(array, "aux", [(i, i ^ 1) for i in range(lax.axis_size("aux"))])


def pack_kernel(b_ref, e_ref, out_ref):
    depth = b_ref.shape[0]
    out_ref[:depth] = b_ref[...]
    value = jnp.full((STRIP, b_ref.shape[1]), e_ref[0], jnp.float32)
    high = value.astype(jnp.bfloat16)
    rest = value - high.astype(jnp.float32)
    middle = rest.astype(jnp.bfloat16)
    low = (rest - middle.astype(jnp.float32)).astype(jnp.bfloat16)
    row = lax.broadcasted_iota(jnp.int32, value.shape, 0)
    parts = jnp.where(row == 0, high.astype(jnp.float32),
                      jnp.where(row == 1, middle.astype(jnp.float32), low.astype(jnp.float32)))
    out_ref[depth:] = parts.astype(jnp.bfloat16)


def place():
    index = lax.axis_index("aux")
    return index // 2, index % 2


def integral_kernel(depth, *refs):
    blocks, vir_ref, keep_ref, send_ref, level_ref, column_ref, whole = refs[:5], *refs[5:]
    z, core = place()
    for k, block in enumerate(blocks):
        parts = block[depth:depth + STRIP].astype(jnp.float32)
        level = parts[0:1] + parts[1:2] + parts[2:3]
        level_ref[k:k + 1] = level
        column_ref[k:k + 1] = vir_ref[...] - level
    for r, (first, second) in enumerate(PAIRS):
        whole[...] = lax.dot_general(
            blocks[first][:depth], blocks[second][:depth], (((0,), (0,)), ((), ())),
            preferred_element_type=jnp.float32,
        )
        for k in range(8):
            strip = ((z + k) % 8) * 2
            mine = pl.multiple_of((strip + core) * STRIP, STRIP)
            other = pl.multiple_of((strip + 1 - core) * STRIP, STRIP)
            rows = slice(r * STRIP, (r + 1) * STRIP)
            keep_ref[k, rows] = whole[pl.ds(mine, STRIP)]
            send_ref[k, rows] = whole[pl.ds(other, STRIP)].astype(jnp.bfloat16)


def pair_sum_kernel(keep_ref, got_ref, own_ref, *out_refs):
    own_ref[...] = keep_ref[0] + got_ref[0].astype(jnp.float32)
    for k, out in enumerate(out_refs, 1):
        out[...] = (keep_ref[k] + got_ref[k].astype(jnp.float32)).astype(jnp.bfloat16)


def amplitude_kernel(*refs):
    own_ref, got_refs, (strip_ref, level_ref, column_ref, out_ref) = refs[0], refs[1:8], refs[8:]
    total = own_ref[...]
    for got in got_refs:
        total = total + got[...].astype(jnp.float32)
    for r, (first, second) in enumerate(PAIRS):
        rows = slice(r * STRIP, (r + 1) * STRIP)
        row_energy = strip_ref[...] - level_ref[first:first + 1]
        out_ref[rows] = (total[rows] / (row_energy + column_ref[second:second + 1])).astype(jnp.bfloat16)


def gamma_kernel(depth, *refs):
    blocks, mine, other_ref, outs, whole = refs[:5], refs[5:13], refs[13], refs[14:19], refs[19]
    z, core = place()
    for k in range(8):
        strip = ((z - k + 8) % 8) * 2
        here = pl.multiple_of((strip + core) * STRIP, STRIP)
        there = pl.multiple_of((strip + 1 - core) * STRIP, STRIP)
        for r in range(len(PAIRS)):
            rows = slice(r * STRIP, (r + 1) * STRIP)
            whole[r, pl.ds(here, STRIP)] = mine[k][rows]
            whole[r, pl.ds(there, STRIP)] = other_ref[k, rows]
    for held, out in enumerate(outs):
        total = None
        for r, (first, second) in enumerate(PAIRS):
            if first == held:
                term = lax.dot_general(
                    blocks[second][:depth], whole[r], (((1,), (1,)), ((), ())), preferred_element_type=jnp.float32
                )
                total = term if total is None else total + term
            if second == held and (first, second) not in ONE_WAY:
                term = lax.dot_general(
                    blocks[first][:depth], whole[r], (((1,), (0,)), ((), ())), preferred_element_type=jnp.float32
                )
                total = term if total is None else total + term
        out[...] = total.astype(out.dtype)


def total_kernel(own_ref, *refs):
    total = own_ref[...]
    for got in refs[:-1]:
        total = total + got[...].astype(jnp.float32)
    refs[-1][...] = total


def call(kernel, ins, out_shape, scratch=()):
    return pl.pallas_call(
        kernel,
        out_shape=out_shape,
        in_specs=ins,
        out_specs=jax.tree.map(lambda _: VMEM, out_shape),
        scratch_shapes=list(scratch),
    )


def body(b_factors, occ_energy, vir_energy):
    f32, bf16 = jnp.float32, jnp.bfloat16
    shape = jax.ShapeDtypeStruct
    columns = b_factors.T
    depth, width = columns.shape
    rows = len(PAIRS) * STRIP

    packed = call(pack_kernel, [VMEM, SMEM], shape((depth + STRIP, width), bf16))(columns, occ_energy)
    blocks = [packed] + [rotate(packed, "occ", -s) for s in HELD[1:]]

    keep, send, level, column = call(
        functools.partial(integral_kernel, depth),
        [VMEM] * 6,
        [shape((8, rows, width), f32), shape((8, rows, width), bf16), shape((8, width), f32), shape((8, width), f32)],
        [pltpu.VMEM((width, width), f32)],
    )(*blocks, vir_energy[None, :])

    pieces = call(
        pair_sum_kernel, [VMEM] * 2, [shape((rows, width), f32)] + [shape((rows, width), bf16)] * 7
    )(keep, sibling(send))
    got = [rotate(pieces[k], "aux", 2 * k) for k in range(1, 8)]

    own_rows = lax.dynamic_slice_in_dim(vir_energy, lax.axis_index("aux") * STRIP, STRIP)
    amplitude = call(amplitude_kernel, [VMEM] * 11, shape((rows, width), bf16))(
        pieces[0], *got, jnp.broadcast_to(own_rows[:, None], (STRIP, width)), level, column
    )
    mine = [amplitude] + [rotate(amplitude, "aux", 2 * k) for k in range(1, 8)]
    other = sibling(jnp.stack(mine))

    parts = call(
        functools.partial(gamma_kernel, depth),
        [VMEM] * 14,
        [shape((depth, width), f32)] + [shape((depth, width), bf16)] * 4,
        [pltpu.VMEM((len(PAIRS), width, width), bf16)],
    )(*blocks, *mine, other)

    back = [rotate(part, "occ", s) for part, s in zip(parts[1:], HELD[1:])]
    return call(total_kernel, [VMEM] * 5, shape((depth, width), f32))(parts[0], *back).T


def solution(mesh):
    placed = (P("occ", "aux"), P("occ"), P())
    return jax.shard_map(
        body, mesh=mesh, in_specs=placed, out_specs=P("occ", "aux"), check_vma=False
    )
```

```python
import functools

import jax
import jax.numpy as jnp
from jax import lax
from jax.experimental import pallas as pl
from jax.experimental.pallas import tpu as pltpu
from jax.sharding import PartitionSpec as P

HELD = (0, 1, 12, 3, 11)
PAIRS = ((0, 0), (0, 1), (0, 2), (1, 2), (3, 1), (0, 3), (1, 4), (3, 2), (3, 4))
ONE_WAY = ((0, 0), (3, 4))
HALF = 16
CHIP = 2 * HALF
SIZE = len(PAIRS) * HALF
VMEM = pl.BlockSpec(memory_space=pltpu.VMEM)
SMEM = pl.BlockSpec(memory_space=pltpu.SMEM)


def send_home(array, by):
    return lax.ppermute(array, "occ", [(i, (i + by) % 16) for i in range(16)])


def along_z(array, hops):
    def target(i):
        return (i // 2 + (hops if i % 2 == 0 else -hops)) % 8 * 2 + i % 2

    return lax.ppermute(array, "aux", [(i, target(i)) for i in range(16)])


def sibling(array):
    return lax.ppermute(array, "aux", [(i, i ^ 1) for i in range(16)])


def place():
    index = lax.axis_index("aux")
    return index // 2, index % 2


def rows_of(chip, half=0):
    return pl.multiple_of((chip + 8) % 8 * CHIP + half * HALF, HALF)


def pack_kernel(b_ref, e_ref, vir_ref, out_ref, row_ref, strip_ref, turned):
    depth, width = b_ref.shape
    out_ref[:depth] = b_ref[...]
    value = jnp.full((HALF, width), e_ref[0], jnp.float32)
    high = value.astype(jnp.bfloat16)
    rest = value - high.astype(jnp.float32)
    middle = rest.astype(jnp.bfloat16)
    low = (rest - middle.astype(jnp.float32)).astype(jnp.bfloat16)
    row = lax.broadcasted_iota(jnp.int32, value.shape, 0)
    parts = jnp.where(row == 0, high.astype(jnp.float32),
                      jnp.where(row == 1, middle.astype(jnp.float32), low.astype(jnp.float32)))
    out_ref[depth:] = parts.astype(jnp.bfloat16)
    row_ref[...] = jnp.broadcast_to(vir_ref[...], row_ref.shape)
    turned[...] = jnp.broadcast_to(vir_ref[...], (width, width)).T
    z, core = place()
    strip_ref[:HALF] = turned[pl.ds(rows_of(z, core), HALF)]
    strip_ref[HALF:] = turned[pl.ds(rows_of(z, 1 - core), HALF)]


def integral_kernel(depth, *refs):
    blocks, row_ref, keep_ref, send_ref, level_ref, column_ref, whole = refs[:5], *refs[5:]
    z, core = place()
    way = 1 - 2 * core
    for k, block in enumerate(blocks):
        parts = block[depth:depth + HALF].astype(jnp.float32)
        level = parts[0:1] + parts[1:2] + parts[2:3]
        level_ref[k:k + 1] = level
        column_ref[k:k + 1] = row_ref[0:1] - level
    for r, (first, second) in enumerate(PAIRS):
        whole[...] = lax.dot_general(
            blocks[first][:depth], blocks[second][:depth], (((0,), (0,)), ((), ())),
            preferred_element_type=jnp.float32,
        )
        for k, (hops, side) in enumerate(((1, 0), (1, 1), (2, 0), (2, 1), (3, 0), (3, 1), (4, 0), (0, 0))):
            to = slice(k * SIZE + r * HALF, k * SIZE + (r + 1) * HALF)
            mine, other = (core, 1 - core) if side == 0 else (1 - core, core)
            keep_ref[to] = whole[pl.ds(rows_of(z + way * hops, mine), HALF)]
            send_ref[to] = whole[pl.ds(rows_of(z - way * hops, other), HALF)].astype(jnp.bfloat16)


def core_sum_kernel(keep_ref, got_ref, *out_refs):
    base = 0
    for out in out_refs:
        rows = slice(base, base + out.shape[0])
        out[...] = (keep_ref[rows] + got_ref[rows].astype(jnp.float32)).astype(out.dtype)
        base += out.shape[0]


def relay_kernel(own_ref, three_ref, four_ref, out_ref):
    total = own_ref[...] + three_ref[...].astype(jnp.float32)
    out_ref[:SIZE] = (total[:SIZE] + four_ref[...].astype(jnp.float32)).astype(out_ref.dtype)
    out_ref[SIZE:] = total[SIZE:].astype(out_ref.dtype)


def chip_sum_kernel(own_ref, one_ref, two_ref, out_ref):
    total = one_ref[...].astype(jnp.float32) + two_ref[...].astype(jnp.float32)
    out_ref[:SIZE] = total[:SIZE] + own_ref[...]
    out_ref[SIZE:] = total[SIZE:]


def amplitude_kernel(mine_ref, other_ref, strip_ref, level_ref, column_ref, out_ref):
    for r, (first, second) in enumerate(PAIRS):
        row_energy = strip_ref[...] - level_ref[first:first + 1]
        denominator = row_energy + column_ref[second:second + 1]
        here, there = slice(r * HALF, (r + 1) * HALF), slice(SIZE + r * HALF, SIZE + (r + 1) * HALF)
        out_ref[here] = ((mine_ref[here] + other_ref[there]) / denominator[:HALF]).astype(jnp.bfloat16)
        out_ref[there] = ((mine_ref[there] + other_ref[here]) / denominator[HALF:]).astype(jnp.bfloat16)


def gamma_kernel(depth, *refs):
    blocks, own, mine, other, outs, whole = refs[:5], refs[5], refs[6:10], refs[10:14], refs[14:19], refs[19]
    z, core = place()
    way = 1 - 2 * core
    for r in range(len(PAIRS)):
        for ref, chip, half in (
            [(own, z, core)]
            + [(ref, z - way * hops, core) for hops, ref in enumerate(mine, 1)]
            + [(ref, z + way * hops, 1 - core) for hops, ref in enumerate(other, 1)]
        ):
            whole[r, pl.ds(rows_of(chip, half), HALF)] = ref[r * HALF:(r + 1) * HALF]
            if ref.shape[0] > SIZE:
                whole[r, pl.ds(rows_of(chip, 1 - half), HALF)] = ref[SIZE + r * HALF:SIZE + (r + 1) * HALF]
    for held, out in enumerate(outs):
        total = None
        for r, (first, second) in enumerate(PAIRS):
            if first == held:
                term = lax.dot_general(
                    blocks[second][:depth], whole[r], (((1,), (1,)), ((), ())), preferred_element_type=jnp.float32
                )
                total = term if total is None else total + term
            if second == held and (first, second) not in ONE_WAY:
                term = lax.dot_general(
                    blocks[first][:depth], whole[r], (((1,), (0,)), ((), ())), preferred_element_type=jnp.float32
                )
                total = term if total is None else total + term
        out[...] = total.astype(out.dtype)


def total_kernel(own_ref, *refs):
    total = own_ref[...]
    for got in refs[:-1]:
        total = total + got[...].astype(jnp.float32)
    refs[-1][...] = total


def call(kernel, ins, out_shape, scratch=()):
    return pl.pallas_call(
        kernel,
        out_shape=out_shape,
        in_specs=ins,
        out_specs=jax.tree.map(lambda _: VMEM, out_shape),
        scratch_shapes=list(scratch),
        compiler_params=pltpu.CompilerParams(vmem_limit_bytes=16 * 1024 * 1024),
    )


def body(b_factors, occ_energy, vir_energy):
    f32, bf16 = jnp.float32, jnp.bfloat16
    shape = jax.ShapeDtypeStruct
    columns = b_factors.T
    depth, width = columns.shape
    square = pltpu.VMEM((width, width), f32)

    packed, row, strip = call(
        pack_kernel, [VMEM, SMEM, VMEM],
        [shape((depth + HALF, width), bf16), shape((8, width), f32), shape((CHIP, width), f32)], [square],
    )(columns, occ_energy, vir_energy[None, :])
    blocks = [packed] + [send_home(packed, -s) for s in HELD[1:]]

    keep, send, level, column = call(
        functools.partial(integral_kernel, depth), [VMEM] * 6,
        [shape((8 * SIZE, width), f32), shape((8 * SIZE, width), bf16)] + [shape((8, width), f32)] * 2, [square],
    )(*blocks, row)
    one, two, three, four, own = call(
        core_sum_kernel, [VMEM] * 2,
        [shape((n * SIZE, width), t) for n, t in ((2, bf16), (2, f32), (2, bf16), (1, bf16), (1, f32))],
    )(keep, sibling(send))
    four = along_z(four, 2)
    three = along_z(three, 1)
    one = along_z(one, 1)
    two = along_z(call(relay_kernel, [VMEM] * 3, shape((2 * SIZE, width), bf16))(two, three, four), 2)
    partial = call(chip_sum_kernel, [VMEM] * 3, shape((2 * SIZE, width), f32))(own, one, two)

    amplitude = call(amplitude_kernel, [VMEM] * 5, shape((2 * SIZE, width), bf16))(
        partial, sibling(partial), strip, level, column
    )
    two = along_z(amplitude, 2)
    one = along_z(amplitude, 1)
    three = along_z(two, 1)
    four = along_z(two[:SIZE], 2)
    mine = [one, two, three, four]
    other = [sibling(piece) for piece in mine]

    parts = call(
        functools.partial(gamma_kernel, depth),
        [VMEM] * 14,
        [shape((depth, width), f32)] + [shape((depth, width), bf16)] * 4,
        [pltpu.VMEM((len(PAIRS), width, width), bf16)],
    )(*blocks, amplitude, *mine, *other)

    back = [send_home(parts[k], HELD[k]) for k in (3, 4, 2, 1)]
    return call(total_kernel, [VMEM] * 5, shape((depth, width), f32))(parts[0], *back).T


def solution(mesh):
    placed = (P("occ", "aux"), P("occ"), P())
    return jax.shard_map(
        body, mesh=mesh, in_specs=placed, out_specs=P("occ", "aux"), check_vma=False
    )
```

```python
import functools

import jax
import jax.numpy as jnp
from jax import lax
from jax.experimental import pallas as pl
from jax.experimental.pallas import tpu as pltpu
from jax.sharding import PartitionSpec as P

HELD = (0, 1, 12, 3, 9)
PAIRS = ((0, 0), (0, 1), (0, 2), (1, 2), (1, 3), (0, 3), (3, 4), (0, 4), (1, 4))
ONE_WAY = ((0, 0), (1, 4))
HALF = 16
CHIP = 2 * HALF
SIZE = len(PAIRS) * HALF
VMEM = pl.BlockSpec(memory_space=pltpu.VMEM)
SMEM = pl.BlockSpec(memory_space=pltpu.SMEM)


def send_home(array, by):
    return lax.ppermute(array, "occ", [(i, (i + by) % 16) for i in range(16)])


def along_z(array, hops):
    def target(i):
        return (i // 2 + (hops if i % 2 == 0 else -hops)) % 8 * 2 + i % 2

    return lax.ppermute(array, "aux", [(i, target(i)) for i in range(16)])


def sibling(array):
    return lax.ppermute(array, "aux", [(i, i ^ 1) for i in range(16)])


def place():
    index = lax.axis_index("aux")
    return index // 2, index % 2


def rows_of(chip, half=0):
    return pl.multiple_of((chip + 8) % 8 * CHIP + half * HALF, HALF)


def pack_kernel(b_ref, e_ref, out_ref):
    depth, width = b_ref.shape
    out_ref[:depth] = b_ref[...]
    value = jnp.full((HALF, width), e_ref[0], jnp.float32)
    high = value.astype(jnp.bfloat16)
    rest = value - high.astype(jnp.float32)
    middle = rest.astype(jnp.bfloat16)
    low = (rest - middle.astype(jnp.float32)).astype(jnp.bfloat16)
    row = lax.broadcasted_iota(jnp.int32, value.shape, 0)
    parts = jnp.where(row == 0, high.astype(jnp.float32),
                      jnp.where(row == 1, middle.astype(jnp.float32), low.astype(jnp.float32)))
    out_ref[depth:] = parts.astype(jnp.bfloat16)


def strip_kernel(vir_ref, row_ref, strip_ref, turned):
    row_ref[...] = jnp.broadcast_to(vir_ref[...], row_ref.shape)
    turned[...] = jnp.broadcast_to(vir_ref[...], turned.shape).T
    z, core = place()
    strip_ref[:HALF] = turned[pl.ds(rows_of(z, core), HALF)]
    strip_ref[HALF:] = turned[pl.ds(rows_of(z, 1 - core), HALF)]


def integral_kernel(depth, *refs):
    blocks, keep_ref, send_ref, whole = refs[:5], *refs[5:]
    z, core = place()
    way = 1 - 2 * core
    for r, (first, second) in enumerate(PAIRS):
        whole[...] = lax.dot_general(
            blocks[first][:depth], blocks[second][:depth], (((0,), (0,)), ((), ())),
            preferred_element_type=jnp.float32,
        )
        for k, (hops, side) in enumerate(((1, 0), (1, 1), (2, 0), (2, 1), (3, 0), (3, 1), (4, 0), (0, 0))):
            to = slice(k * SIZE + r * HALF, k * SIZE + (r + 1) * HALF)
            mine, other = (core, 1 - core) if side == 0 else (1 - core, core)
            keep_ref[to] = whole[pl.ds(rows_of(z + way * hops, mine), HALF)]
            send_ref[to] = whole[pl.ds(rows_of(z - way * hops, other), HALF)].astype(jnp.bfloat16)


def core_sum_kernel(keep_ref, got_ref, *out_refs):
    base = 0
    for out in out_refs:
        rows = slice(base, base + out.shape[0])
        out[...] = (keep_ref[rows] + got_ref[rows].astype(jnp.float32)).astype(out.dtype)
        base += out.shape[0]


def relay_kernel(own_ref, three_ref, four_ref, out_ref):
    total = own_ref[...] + three_ref[...].astype(jnp.float32)
    out_ref[:SIZE] = (total[:SIZE] + four_ref[...].astype(jnp.float32)).astype(out_ref.dtype)
    out_ref[SIZE:] = total[SIZE:].astype(out_ref.dtype)


def chip_sum_kernel(own_ref, one_ref, two_ref, out_ref):
    total = one_ref[...].astype(jnp.float32) + two_ref[...].astype(jnp.float32)
    out_ref[:SIZE] = total[:SIZE] + own_ref[...]
    out_ref[SIZE:] = total[SIZE:]


def amplitude_kernel(depth, *refs):
    blocks, mine_ref, other_ref, row_ref, strip_ref, out_ref = refs[:5], *refs[5:]
    levels = []
    for block in blocks:
        parts = block[depth:depth + HALF].astype(jnp.float32)
        levels.append(parts[0:1] + parts[1:2] + parts[2:3])
    for r, (first, second) in enumerate(PAIRS):
        denominator = (strip_ref[...] - levels[first]) + (row_ref[0:1] - levels[second])
        here, there = slice(r * HALF, (r + 1) * HALF), slice(SIZE + r * HALF, SIZE + (r + 1) * HALF)
        out_ref[here] = ((mine_ref[here] + other_ref[there]) / denominator[:HALF]).astype(jnp.bfloat16)
        out_ref[there] = ((mine_ref[there] + other_ref[here]) / denominator[HALF:]).astype(jnp.bfloat16)


def gamma_kernel(depth, *refs):
    blocks, own, mine, other, outs, whole = refs[:5], refs[5], refs[6:10], refs[10:14], refs[14:18], refs[18]
    z, core = place()
    way = 1 - 2 * core
    for r in range(len(PAIRS)):
        for ref, chip, half in (
            [(own, z, core)]
            + [(ref, z - way * hops, core) for hops, ref in enumerate(mine, 1)]
            + [(ref, z + way * hops, 1 - core) for hops, ref in enumerate(other, 1)]
        ):
            whole[r, pl.ds(rows_of(chip, half), HALF)] = ref[r * HALF:(r + 1) * HALF]
            if ref.shape[0] > SIZE:
                whole[r, pl.ds(rows_of(chip, 1 - half), HALF)] = ref[SIZE + r * HALF:SIZE + (r + 1) * HALF]
    gammas(depth, blocks, range(1, 5), whole, outs)


def own_kernel(depth, *refs):
    gammas(depth, refs[:5], (0,), refs[5], refs[6:])


def gammas(depth, blocks, held_blocks, whole, outs):
    for held, out in zip(held_blocks, outs):
        total = None
        for r, (first, second) in enumerate(PAIRS):
            if first == held:
                term = lax.dot_general(
                    blocks[second][:depth], whole[r], (((1,), (1,)), ((), ())), preferred_element_type=jnp.float32
                )
                total = term if total is None else total + term
            if second == held and (first, second) not in ONE_WAY:
                term = lax.dot_general(
                    blocks[first][:depth], whole[r], (((1,), (0,)), ((), ())), preferred_element_type=jnp.float32
                )
                total = term if total is None else total + term
        out[...] = total.astype(out.dtype)


def total_kernel(own_ref, *refs):
    total = own_ref[...]
    for got in refs[:-1]:
        total = total + got[...].astype(jnp.float32)
    refs[-1][...] = total


def call(kernel, ins, out_shape, scratch=()):
    return pl.pallas_call(
        kernel,
        out_shape=out_shape,
        in_specs=ins,
        out_specs=jax.tree.map(lambda _: VMEM, out_shape),
        scratch_shapes=list(scratch),
        compiler_params=pltpu.CompilerParams(vmem_limit_bytes=16 * 1024 * 1024),
    )


def body(b_factors, occ_energy, vir_energy):
    f32, bf16 = jnp.float32, jnp.bfloat16
    shape = jax.ShapeDtypeStruct
    columns = b_factors.T
    depth, width = columns.shape
    square = pltpu.VMEM((width, width), f32)

    packed = call(pack_kernel, [VMEM, SMEM], shape((depth + HALF, width), bf16))(columns, occ_energy)
    blocks = [packed] + [send_home(packed, -s) for s in HELD[1:]]

    row, strip = call(strip_kernel, [VMEM], [shape((8, width), f32), shape((CHIP, width), f32)], [square])(
        vir_energy[None, :]
    )

    keep, send = call(
        functools.partial(integral_kernel, depth), [VMEM] * 5,
        [shape((8 * SIZE, width), f32), shape((8 * SIZE, width), bf16)], [square],
    )(*blocks)
    one, two, three, four, own = call(
        core_sum_kernel, [VMEM] * 2,
        [shape((n * SIZE, width), t) for n, t in ((2, bf16), (2, f32), (2, bf16), (1, bf16), (1, f32))],
    )(keep, sibling(send))
    four = along_z(four, 2)
    three = along_z(three, 1)
    one = along_z(one, 1)
    two = along_z(call(relay_kernel, [VMEM] * 3, shape((2 * SIZE, width), bf16))(two, three, four), 2)
    partial = call(chip_sum_kernel, [VMEM] * 3, shape((2 * SIZE, width), f32))(own, one, two)

    amplitude = call(functools.partial(amplitude_kernel, depth), [VMEM] * 9, shape((2 * SIZE, width), bf16))(
        *blocks, partial, sibling(partial), row, strip
    )
    two = along_z(amplitude, 2)
    one = along_z(amplitude, 1)
    three = along_z(two, 1)
    four = along_z(two[:SIZE], 2)
    mine = [one, two, three, four]
    other = [sibling(piece) for piece in mine]

    parts = call(
        functools.partial(gamma_kernel, depth),
        [VMEM] * 14,
        [shape((depth, width), bf16)] * 4 + [shape((len(PAIRS), width, width), bf16)],
    )(*blocks, amplitude, *mine, *other)
    *parts, whole = parts
    own = call(functools.partial(own_kernel, depth), [VMEM] * 6, [shape((depth, width), f32)])(*blocks, whole)[0]

    back = [send_home(parts[k - 1], HELD[k]) for k in (4, 3, 2, 1)]
    return call(total_kernel, [VMEM] * 5, shape((depth, width), f32))(own, *back).T


def solution(mesh):
    placed = (P("occ", "aux"), P("occ"), P())
    return jax.shard_map(
        body, mesh=mesh, in_specs=placed, out_specs=P("occ", "aux"), check_vma=False
    )
```

```python
import functools

import jax
import jax.numpy as jnp
from jax import lax
from jax.experimental import pallas as pl
from jax.experimental.pallas import tpu as pltpu
from jax.sharding import PartitionSpec as P

HELD = (0, 1, 12, 3, 9)
PAIRS = ((0, 0), (0, 3), (3, 4), (0, 4), (0, 1), (0, 2), (1, 2), (1, 3), (1, 4))
EARLY = 4
ONE_WAY = ((0, 0), (1, 4))
HALF = 16
CHIP = 2 * HALF
SIZE = len(PAIRS) * HALF
VMEM = pl.BlockSpec(memory_space=pltpu.VMEM)
SMEM = pl.BlockSpec(memory_space=pltpu.SMEM)


def send_home(array, by):
    return lax.ppermute(array, "occ", [(i, (i + by) % 16) for i in range(16)])


def along_z(array, hops):
    def target(i):
        return (i // 2 + (hops if i % 2 == 0 else -hops)) % 8 * 2 + i % 2

    return lax.ppermute(array, "aux", [(i, target(i)) for i in range(16)])


def sibling(array):
    return lax.ppermute(array, "aux", [(i, i ^ 1) for i in range(16)])


def place():
    index = lax.axis_index("aux")
    return index // 2, index % 2


def rows_of(chip, half=0):
    return pl.multiple_of((chip + 8) % 8 * CHIP + half * HALF, HALF)


def pack_kernel(b_ref, e_ref, out_ref):
    depth, width = b_ref.shape
    out_ref[:depth] = b_ref[...]
    value = jnp.full((HALF, width), e_ref[0], jnp.float32)
    high = value.astype(jnp.bfloat16)
    rest = value - high.astype(jnp.float32)
    middle = rest.astype(jnp.bfloat16)
    low = (rest - middle.astype(jnp.float32)).astype(jnp.bfloat16)
    row = lax.broadcasted_iota(jnp.int32, value.shape, 0)
    parts = jnp.where(row == 0, high.astype(jnp.float32),
                      jnp.where(row == 1, middle.astype(jnp.float32), low.astype(jnp.float32)))
    out_ref[depth:] = parts.astype(jnp.bfloat16)


def strip_kernel(vir_ref, row_ref, strip_ref, turned):
    row_ref[...] = jnp.broadcast_to(vir_ref[...], row_ref.shape)
    turned[...] = jnp.broadcast_to(vir_ref[...], turned.shape).T
    z, core = place()
    strip_ref[:HALF] = turned[pl.ds(rows_of(z, core), HALF)]
    strip_ref[HALF:] = turned[pl.ds(rows_of(z, 1 - core), HALF)]


def integrals(depth, blocks, pairs, keep_ref, send_ref, whole, size):
    z, core = place()
    way = 1 - 2 * core
    turned = {first: blocks[first][:depth].T for first in {PAIRS[r][0]: None for r in pairs}}
    for r in pairs:
        first, second = PAIRS[r]
        whole[...] = jnp.dot(turned[first], blocks[second][:depth], preferred_element_type=jnp.float32)
        for k, (hops, side) in enumerate(((1, 0), (1, 1), (2, 0), (2, 1), (3, 0), (3, 1), (4, 0), (0, 0))):
            to = slice(k * size + r * HALF, k * size + (r + 1) * HALF)
            mine, other = (core, 1 - core) if side == 0 else (1 - core, core)
            keep_ref[to] = whole[pl.ds(rows_of(z + way * hops, mine), HALF)]
            send_ref[to] = whole[pl.ds(rows_of(z - way * hops, other), HALF)].astype(jnp.bfloat16)


def early_kernel(depth, own_ref, third_ref, fourth_ref, keep_ref, send_ref, whole):
    integrals(depth, {0: own_ref, 3: third_ref, 4: fourth_ref}, range(EARLY), keep_ref, send_ref, whole, EARLY * HALF)


def late_kernel(depth, *refs):
    early_keep, early_send, keep_ref, send_ref, whole = refs[5:]
    size = EARLY * HALF
    for k in range(8):
        keep_ref[k * SIZE:k * SIZE + size] = early_keep[k * size:(k + 1) * size]
        send_ref[k * SIZE:k * SIZE + size] = early_send[k * size:(k + 1) * size]
    integrals(depth, refs[:5], range(EARLY, len(PAIRS)), keep_ref, send_ref, whole, SIZE)


def core_sum_kernel(keep_ref, got_ref, *out_refs):
    base = 0
    for out in out_refs:
        rows = slice(base, base + out.shape[0])
        out[...] = (keep_ref[rows] + got_ref[rows].astype(jnp.float32)).astype(out.dtype)
        base += out.shape[0]


def relay_kernel(own_ref, three_ref, four_ref, out_ref):
    total = own_ref[...] + three_ref[...].astype(jnp.float32)
    out_ref[:SIZE] = (total[:SIZE] + four_ref[...].astype(jnp.float32)).astype(out_ref.dtype)
    out_ref[SIZE:] = total[SIZE:].astype(out_ref.dtype)


def chip_sum_kernel(own_ref, one_ref, two_ref, out_ref):
    total = one_ref[...].astype(jnp.float32) + two_ref[...].astype(jnp.float32)
    out_ref[:SIZE] = total[:SIZE] + own_ref[...]
    out_ref[SIZE:] = total[SIZE:]


def amplitude_kernel(depth, *refs):
    blocks, mine_ref, other_ref, row_ref, strip_ref, out_ref = refs[:5], *refs[5:]
    levels = []
    for block in blocks:
        parts = block[depth:depth + HALF].astype(jnp.float32)
        levels.append(parts[0:1] + parts[1:2] + parts[2:3])
    for r, (first, second) in enumerate(PAIRS):
        denominator = (strip_ref[...] - levels[first]) + (row_ref[0:1] - levels[second])
        here, there = slice(r * HALF, (r + 1) * HALF), slice(SIZE + r * HALF, SIZE + (r + 1) * HALF)
        out_ref[here] = ((mine_ref[here] + other_ref[there]) / denominator[:HALF]).astype(jnp.bfloat16)
        out_ref[there] = ((mine_ref[there] + other_ref[here]) / denominator[HALF:]).astype(jnp.bfloat16)


def gamma_kernel(depth, *refs):
    blocks, own, mine, other, outs, whole = refs[:5], refs[5], refs[6:10], refs[10:14], refs[14:18], refs[18]
    z, core = place()
    way = 1 - 2 * core
    for r in range(len(PAIRS)):
        for ref, chip, half in (
            [(own, z, core)]
            + [(ref, z - way * hops, core) for hops, ref in enumerate(mine, 1)]
            + [(ref, z + way * hops, 1 - core) for hops, ref in enumerate(other, 1)]
        ):
            whole[r, pl.ds(rows_of(chip, half), HALF)] = ref[r * HALF:(r + 1) * HALF]
            if ref.shape[0] > SIZE:
                whole[r, pl.ds(rows_of(chip, 1 - half), HALF)] = ref[SIZE + r * HALF:SIZE + (r + 1) * HALF]
    gammas(depth, blocks, range(1, 5), whole, outs)


def own_kernel(depth, *refs):
    gammas(depth, refs[:5], (0,), refs[5], refs[6:])


def gammas(depth, blocks, held_blocks, whole, outs):
    for held, out in zip(held_blocks, outs):
        total = None
        for r, (first, second) in enumerate(PAIRS):
            if first == held:
                term = lax.dot_general(
                    blocks[second][:depth], whole[r], (((1,), (1,)), ((), ())), preferred_element_type=jnp.float32
                )
                total = term if total is None else total + term
            if second == held and (first, second) not in ONE_WAY:
                term = lax.dot_general(
                    blocks[first][:depth], whole[r], (((1,), (0,)), ((), ())), preferred_element_type=jnp.float32
                )
                total = term if total is None else total + term
        out[...] = total.astype(out.dtype)


def call(kernel, ins, out_shape, scratch=()):
    return pl.pallas_call(
        kernel,
        out_shape=out_shape,
        in_specs=ins,
        out_specs=jax.tree.map(lambda _: VMEM, out_shape),
        scratch_shapes=list(scratch),
        compiler_params=pltpu.CompilerParams(vmem_limit_bytes=16 * 1024 * 1024),
    )


def body(b_factors, occ_energy, vir_energy):
    f32, bf16 = jnp.float32, jnp.bfloat16
    shape = jax.ShapeDtypeStruct
    columns = b_factors.T
    depth, width = columns.shape
    square = pltpu.VMEM((width, width), f32)

    packed = call(pack_kernel, [VMEM, SMEM], shape((depth + HALF, width), bf16))(columns, occ_energy)
    blocks = [packed] + [send_home(packed, -s) for s in HELD[1:]]

    row, strip = call(strip_kernel, [VMEM], [shape((8, width), f32), shape((CHIP, width), f32)], [square])(
        vir_energy[None, :]
    )

    def halves(pairs):
        return [shape((8 * pairs * HALF, width), f32), shape((8 * pairs * HALF, width), bf16)]

    early = call(functools.partial(early_kernel, depth), [VMEM] * 3, halves(EARLY), [square])(
        blocks[0], blocks[3], blocks[4]
    )
    keep, send = call(functools.partial(late_kernel, depth), [VMEM] * 7, halves(len(PAIRS)), [square])(*blocks, *early)
    one, two, three, four, own = call(
        core_sum_kernel, [VMEM] * 2,
        [shape((n * SIZE, width), t) for n, t in ((2, bf16), (2, f32), (2, bf16), (1, bf16), (1, f32))],
    )(keep, sibling(send))
    four = along_z(four, 2)
    three = along_z(three, 1)
    one = along_z(one, 1)
    two = along_z(call(relay_kernel, [VMEM] * 3, shape((2 * SIZE, width), bf16))(two, three, four), 2)
    partial = call(chip_sum_kernel, [VMEM] * 3, shape((2 * SIZE, width), f32))(own, one, two)

    amplitude = call(functools.partial(amplitude_kernel, depth), [VMEM] * 9, shape((2 * SIZE, width), bf16))(
        *blocks, partial, sibling(partial), row, strip
    )
    two = along_z(amplitude, 2)
    one = along_z(amplitude, 1)
    three = along_z(two, 1)
    four = along_z(two[:SIZE], 2)
    mine = [one, two, three, four]
    other = [sibling(piece) for piece in mine]

    parts = call(
        functools.partial(gamma_kernel, depth),
        [VMEM] * 14,
        [shape((depth, width), bf16)] * 4 + [shape((len(PAIRS), width, width), bf16)],
    )(*blocks, amplitude, *mine, *other)
    *parts, whole = parts
    own = call(functools.partial(own_kernel, depth), [VMEM] * 6, [shape((depth, width), f32)])(*blocks, whole)[0]

    back = [send_home(parts[k - 1], HELD[k]) for k in (4, 3, 2, 1)]
    for part in back:
        own = own + part.astype(f32)
    return own.T


def solution(mesh):
    placed = (P("occ", "aux"), P("occ"), P())
    return jax.shard_map(
        body, mesh=mesh, in_specs=placed, out_specs=P("occ", "aux"), check_vma=False
    )
```

```python
import functools

import jax
import jax.numpy as jnp
from jax import lax
from jax.experimental import pallas as pl
from jax.experimental.pallas import tpu as pltpu
from jax.sharding import PartitionSpec as P

HELD = (0, 1, 12, 3, 9)
PAIRS = ((0, 0), (0, 3), (3, 4), (0, 4), (0, 1), (0, 2), (1, 2), (1, 3), (1, 4))
EARLY = 4
ONE_WAY = ((0, 0), (1, 4))
HALF = 16
CHIP = 2 * HALF
SIZE = len(PAIRS) * HALF
VMEM = pl.BlockSpec(memory_space=pltpu.VMEM)
SMEM = pl.BlockSpec(memory_space=pltpu.SMEM)


def send_home(array, by):
    return lax.ppermute(array, "occ", [(i, (i + by) % 16) for i in range(16)])


def along_z(array, hops):
    def target(i):
        return (i // 2 + (hops if i % 2 == 0 else -hops)) % 8 * 2 + i % 2

    return lax.ppermute(array, "aux", [(i, target(i)) for i in range(16)])


def sibling(array):
    return lax.ppermute(array, "aux", [(i, i ^ 1) for i in range(16)])


def place():
    index = lax.axis_index("aux")
    return index // 2, index % 2


def rows_of(chip, half=0):
    return pl.multiple_of((chip + 8) % 8 * CHIP + half * HALF, HALF)


def pack_kernel(b_ref, e_ref, out_ref):
    depth, width = b_ref.shape
    out_ref[:depth] = b_ref[...]
    value = jnp.full((HALF, width), e_ref[0], jnp.float32)
    high = value.astype(jnp.bfloat16)
    rest = value - high.astype(jnp.float32)
    middle = rest.astype(jnp.bfloat16)
    low = (rest - middle.astype(jnp.float32)).astype(jnp.bfloat16)
    row = lax.broadcasted_iota(jnp.int32, value.shape, 0)
    parts = jnp.where(row == 0, high.astype(jnp.float32),
                      jnp.where(row == 1, middle.astype(jnp.float32), low.astype(jnp.float32)))
    out_ref[depth:] = parts.astype(jnp.bfloat16)


def strip_kernel(vir_ref, row_ref, strip_ref, turned):
    row_ref[...] = jnp.broadcast_to(vir_ref[...], row_ref.shape)
    turned[...] = jnp.broadcast_to(vir_ref[...], turned.shape).T
    z, core = place()
    strip_ref[:HALF] = turned[pl.ds(rows_of(z, core), HALF)]
    strip_ref[HALF:] = turned[pl.ds(rows_of(z, 1 - core), HALF)]


def integrals(depth, blocks, pairs, keep_ref, send_ref, whole, size):
    z, core = place()
    way = 1 - 2 * core
    turned = {first: blocks[first][:depth].T for first in {PAIRS[r][0]: None for r in pairs}}
    for r in pairs:
        first, second = PAIRS[r]
        whole[...] = jnp.dot(turned[first], blocks[second][:depth], preferred_element_type=jnp.float32)
        for k, (hops, side) in enumerate(((1, 0), (1, 1), (2, 0), (2, 1), (3, 0), (3, 1), (4, 0), (0, 0))):
            to = slice(k * size + r * HALF, k * size + (r + 1) * HALF)
            mine, other = (core, 1 - core) if side == 0 else (1 - core, core)
            keep_ref[to] = whole[pl.ds(rows_of(z + way * hops, mine), HALF)]
            send_ref[to] = whole[pl.ds(rows_of(z - way * hops, other), HALF)].astype(jnp.bfloat16)


def early_kernel(depth, own_ref, third_ref, fourth_ref, keep_ref, send_ref, whole):
    integrals(depth, {0: own_ref, 3: third_ref, 4: fourth_ref}, range(EARLY), keep_ref, send_ref, whole, EARLY * HALF)


def late_kernel(depth, *refs):
    early_keep, early_send, keep_ref, send_ref, whole = refs[5:]
    size = EARLY * HALF
    for k in range(8):
        keep_ref[k * SIZE:k * SIZE + size] = early_keep[k * size:(k + 1) * size]
        send_ref[k * SIZE:k * SIZE + size] = early_send[k * size:(k + 1) * size]
    integrals(depth, refs[:5], range(EARLY, len(PAIRS)), keep_ref, send_ref, whole, SIZE)


def core_sum_kernel(keep_ref, got_ref, *out_refs):
    base = 0
    for out in out_refs:
        rows = slice(base, base + out.shape[0])
        out[...] = (keep_ref[rows] + got_ref[rows].astype(jnp.float32)).astype(out.dtype)
        base += out.shape[0]


def relay_kernel(own_ref, three_ref, four_ref, out_ref):
    total = own_ref[...] + three_ref[...].astype(jnp.float32)
    out_ref[:SIZE] = (total[:SIZE] + four_ref[...].astype(jnp.float32)).astype(out_ref.dtype)
    out_ref[SIZE:] = total[SIZE:].astype(out_ref.dtype)


def chip_sum_kernel(own_ref, one_ref, two_ref, out_ref):
    total = one_ref[...].astype(jnp.float32) + two_ref[...].astype(jnp.float32)
    out_ref[:SIZE] = total[:SIZE] + own_ref[...]
    out_ref[SIZE:] = total[SIZE:]


def amplitude_kernel(depth, *refs):
    blocks, mine_ref, other_ref, row_ref, strip_ref, out_ref = refs[:5], *refs[5:]
    levels = []
    for block in blocks:
        parts = block[depth:depth + HALF].astype(jnp.float32)
        levels.append(parts[0:1] + parts[1:2] + parts[2:3])
    for r, (first, second) in enumerate(PAIRS):
        denominator = (strip_ref[...] - levels[first]) + (row_ref[0:1] - levels[second])
        here, there = slice(r * HALF, (r + 1) * HALF), slice(SIZE + r * HALF, SIZE + (r + 1) * HALF)
        out_ref[here] = ((mine_ref[here] + other_ref[there]) / denominator[:HALF]).astype(jnp.bfloat16)
        out_ref[there] = ((mine_ref[there] + other_ref[here]) / denominator[HALF:]).astype(jnp.bfloat16)


def gamma_kernel(depth, *refs):
    blocks, own, mine, other, outs, whole = refs[:5], refs[5], refs[6:10], refs[10:14], refs[14:18], refs[18]
    z, core = place()
    way = 1 - 2 * core
    for r in range(len(PAIRS)):
        for ref, chip, half in (
            [(own, z, core)]
            + [(ref, z - way * hops, core) for hops, ref in enumerate(mine, 1)]
            + [(ref, z + way * hops, 1 - core) for hops, ref in enumerate(other, 1)]
        ):
            whole[r, pl.ds(rows_of(chip, half), HALF)] = ref[r * HALF:(r + 1) * HALF]
            if ref.shape[0] > SIZE:
                whole[r, pl.ds(rows_of(chip, 1 - half), HALF)] = ref[SIZE + r * HALF:SIZE + (r + 1) * HALF]
    gammas(depth, blocks, range(1, 5), whole, outs)


def own_kernel(depth, *refs):
    gammas(depth, refs[:5], (0,), refs[5], refs[6:])


def gammas(depth, blocks, held_blocks, whole, outs):
    for held, out in zip(held_blocks, outs):
        total = None
        for r, (first, second) in enumerate(PAIRS):
            if first == held:
                term = lax.dot_general(
                    blocks[second][:depth], whole[r], (((1,), (1,)), ((), ())), preferred_element_type=jnp.float32
                )
                total = term if total is None else total + term
            if second == held and (first, second) not in ONE_WAY:
                term = lax.dot_general(
                    blocks[first][:depth], whole[r], (((1,), (0,)), ((), ())), preferred_element_type=jnp.float32
                )
                total = term if total is None else total + term
        out[...] = total.astype(out.dtype)


def call(kernel, ins, out_shape, scratch=()):
    return pl.pallas_call(
        kernel,
        out_shape=out_shape,
        in_specs=ins,
        out_specs=jax.tree.map(lambda _: VMEM, out_shape),
        scratch_shapes=list(scratch),
        compiler_params=pltpu.CompilerParams(vmem_limit_bytes=16 * 1024 * 1024),
    )


def body(b_factors, occ_energy, vir_energy):
    f32, bf16 = jnp.float32, jnp.bfloat16
    shape = jax.ShapeDtypeStruct
    columns = b_factors.T
    depth, width = columns.shape
    square = pltpu.VMEM((width, width), f32)

    packed = call(pack_kernel, [VMEM, SMEM], shape((depth + HALF, width), bf16))(columns, occ_energy)
    blocks = [packed] + [send_home(packed, -s) for s in HELD[1:]]

    row, strip = call(strip_kernel, [VMEM], [shape((8, width), f32), shape((CHIP, width), f32)], [square])(
        vir_energy[None, :]
    )

    def halves(pairs):
        return [shape((8 * pairs * HALF, width), f32), shape((8 * pairs * HALF, width), bf16)]

    early = call(functools.partial(early_kernel, depth), [VMEM] * 3, halves(EARLY), [square])(
        blocks[0], blocks[3], blocks[4]
    )
    keep, send = call(functools.partial(late_kernel, depth), [VMEM] * 7, halves(len(PAIRS)), [square])(*blocks, *early)
    one, two, three, four, own = call(
        core_sum_kernel, [VMEM] * 2,
        [shape((n * SIZE, width), t) for n, t in ((2, bf16), (2, f32), (2, bf16), (1, bf16), (1, f32))],
    )(keep, sibling(send))
    four = along_z(four, 2)
    three = along_z(three, 1)
    one = along_z(one, 1)
    two = along_z(call(relay_kernel, [VMEM] * 3, shape((2 * SIZE, width), bf16))(two, three, four), 2)
    partial = call(chip_sum_kernel, [VMEM] * 3, shape((2 * SIZE, width), f32))(own, one, two)

    amplitude = call(functools.partial(amplitude_kernel, depth), [VMEM] * 9, shape((2 * SIZE, width), bf16))(
        *blocks, partial, sibling(partial), row, strip
    )
    two = along_z(amplitude, 2)
    one = along_z(amplitude, 1)
    three = along_z(two, 1)
    four = along_z(two[:SIZE], 2)
    mine = [one, two, three, four]
    other = [sibling(piece) for piece in mine]

    parts = call(
        functools.partial(gamma_kernel, depth),
        [VMEM] * 14,
        [shape((depth, width), bf16)] * 4 + [shape((len(PAIRS), width, width), bf16)],
    )(*blocks, amplitude, *mine, *other)
    *parts, whole = parts
    own = call(functools.partial(own_kernel, depth), [VMEM] * 6, [shape((depth, width), f32)])(*blocks, whole)[0]

    back = [send_home(parts[k - 1], HELD[k]) for k in (4, 3, 1, 2)]
    for part in back:
        own = own + part.astype(f32)
    return own.T


def solution(mesh):
    placed = (P("occ", "aux"), P("occ"), P())
    return jax.shard_map(
        body, mesh=mesh, in_specs=placed, out_specs=P("occ", "aux"), check_vma=False
    )
```

```python
import functools

import jax
import jax.numpy as jnp
from jax import lax
from jax.experimental import pallas as pl
from jax.experimental.pallas import tpu as pltpu
from jax.sharding import PartitionSpec as P

HELD = (0, 1, 12, 3, 9)
PAIRS = ((0, 0), (0, 3), (3, 4), (0, 4), (0, 1), (0, 2), (1, 2), (1, 3), (1, 4))
EARLY = 4
ONE_WAY = ((0, 0), (1, 4))
HALF = 16
CHIP = 2 * HALF
SIZE = len(PAIRS) * HALF
VMEM = pl.BlockSpec(memory_space=pltpu.VMEM)
SMEM = pl.BlockSpec(memory_space=pltpu.SMEM)


def send_home(array, by):
    return lax.ppermute(array, "occ", [(i, (i + by) % 16) for i in range(16)])


def along_z(array, hops):
    def target(i):
        return (i // 2 + (hops if i % 2 == 0 else -hops)) % 8 * 2 + i % 2

    return lax.ppermute(array, "aux", [(i, target(i)) for i in range(16)])


def sibling(array):
    return lax.ppermute(array, "aux", [(i, i ^ 1) for i in range(16)])


def place():
    index = lax.axis_index("aux")
    return index // 2, index % 2


def rows_of(chip, half=0):
    return pl.multiple_of((chip + 8) % 8 * CHIP + half * HALF, HALF)


def pack_kernel(b_ref, e_ref, out_ref):
    depth, width = b_ref.shape
    out_ref[:depth] = b_ref[...]
    value = jnp.full((HALF, width), e_ref[0], jnp.float32)
    high = value.astype(jnp.bfloat16)
    rest = value - high.astype(jnp.float32)
    middle = rest.astype(jnp.bfloat16)
    low = (rest - middle.astype(jnp.float32)).astype(jnp.bfloat16)
    row = lax.broadcasted_iota(jnp.int32, value.shape, 0)
    parts = jnp.where(row == 0, high.astype(jnp.float32),
                      jnp.where(row == 1, middle.astype(jnp.float32), low.astype(jnp.float32)))
    out_ref[depth:] = parts.astype(jnp.bfloat16)


def strip_kernel(vir_ref, row_ref, strip_ref, turned):
    row_ref[...] = jnp.broadcast_to(vir_ref[...], row_ref.shape)
    turned[...] = jnp.broadcast_to(vir_ref[...], turned.shape).T
    z, core = place()
    strip_ref[:HALF] = turned[pl.ds(rows_of(z, core), HALF)]
    strip_ref[HALF:] = turned[pl.ds(rows_of(z, 1 - core), HALF)]


def integrals(depth, blocks, pairs, keep_ref, send_ref, whole, size):
    z, core = place()
    way = 1 - 2 * core
    turned = {first: blocks[first][:depth].T for first in {PAIRS[r][0]: None for r in pairs}}
    for r in pairs:
        first, second = PAIRS[r]
        whole[...] = jnp.dot(turned[first], blocks[second][:depth], preferred_element_type=jnp.float32)
        for k, (hops, side) in enumerate(((1, 0), (1, 1), (2, 0), (2, 1), (3, 0), (3, 1), (4, 0), (0, 0))):
            to = slice(k * size + r * HALF, k * size + (r + 1) * HALF)
            mine, other = (core, 1 - core) if side == 0 else (1 - core, core)
            keep_ref[to] = whole[pl.ds(rows_of(z + way * hops, mine), HALF)]
            send_ref[to] = whole[pl.ds(rows_of(z - way * hops, other), HALF)].astype(jnp.bfloat16)


def early_kernel(depth, own_ref, third_ref, fourth_ref, keep_ref, send_ref, whole):
    integrals(depth, {0: own_ref, 3: third_ref, 4: fourth_ref}, range(EARLY), keep_ref, send_ref, whole, EARLY * HALF)


def late_kernel(depth, *refs):
    early_keep, early_send, keep_ref, send_ref, whole = refs[5:]
    size = EARLY * HALF
    for k in range(8):
        keep_ref[k * SIZE:k * SIZE + size] = early_keep[k * size:(k + 1) * size]
        send_ref[k * SIZE:k * SIZE + size] = early_send[k * size:(k + 1) * size]
    integrals(depth, refs[:5], range(EARLY, len(PAIRS)), keep_ref, send_ref, whole, SIZE)


def core_sum_kernel(keep_ref, got_ref, *out_refs):
    base = 0
    for out in out_refs:
        rows = slice(base, base + out.shape[0])
        out[...] = (keep_ref[rows] + got_ref[rows].astype(jnp.float32)).astype(out.dtype)
        base += out.shape[0]


def relay_kernel(own_ref, three_ref, four_ref, out_ref):
    total = own_ref[...] + three_ref[...].astype(jnp.float32)
    out_ref[:SIZE] = (total[:SIZE] + four_ref[...].astype(jnp.float32)).astype(out_ref.dtype)
    out_ref[SIZE:] = total[SIZE:].astype(out_ref.dtype)


def chip_sum_kernel(own_ref, one_ref, two_ref, out_ref):
    total = one_ref[...].astype(jnp.float32) + two_ref[...].astype(jnp.float32)
    out_ref[:SIZE] = total[:SIZE] + own_ref[...]
    out_ref[SIZE:] = total[SIZE:]


def amplitude_kernel(depth, *refs):
    blocks, mine_ref, other_ref, row_ref, strip_ref, out_ref = refs[:5], *refs[5:]
    levels = []
    for block in blocks:
        parts = block[depth:depth + HALF].astype(jnp.float32)
        levels.append(parts[0:1] + parts[1:2] + parts[2:3])
    for r, (first, second) in enumerate(PAIRS):
        denominator = (strip_ref[...] - levels[first]) + (row_ref[0:1] - levels[second])
        here, there = slice(r * HALF, (r + 1) * HALF), slice(SIZE + r * HALF, SIZE + (r + 1) * HALF)
        out_ref[here] = ((mine_ref[here] + other_ref[there]) / denominator[:HALF]).astype(jnp.bfloat16)
        out_ref[there] = ((mine_ref[there] + other_ref[here]) / denominator[HALF:]).astype(jnp.bfloat16)


def gamma_kernel(depth, *refs):
    blocks, own, mine, other, outs, whole = refs[:5], refs[5], refs[6:10], refs[10:13], refs[13:17], refs[17]
    z, core = place()
    way = 1 - 2 * core
    for r in range(len(PAIRS)):
        for ref, chip, half in (
            [(own, z, core)]
            + [(ref, z - way * hops, core) for hops, ref in enumerate(mine, 1)]
            + [(ref, z + way * hops, 1 - core) for hops, ref in enumerate(other, 1)]
        ):
            whole[r, pl.ds(rows_of(chip, half), HALF)] = ref[r * HALF:(r + 1) * HALF]
            if ref.shape[0] > SIZE:
                whole[r, pl.ds(rows_of(chip, 1 - half), HALF)] = ref[SIZE + r * HALF:SIZE + (r + 1) * HALF]
    gammas(depth, blocks, range(1, 5), whole, outs)


def own_kernel(depth, *refs):
    gammas(depth, refs[:5], (0,), refs[5], refs[6:])


def gammas(depth, blocks, held_blocks, whole, outs):
    for held, out in zip(held_blocks, outs):
        total = None
        for r, (first, second) in enumerate(PAIRS):
            if first == held:
                term = lax.dot_general(
                    blocks[second][:depth], whole[r], (((1,), (1,)), ((), ())), preferred_element_type=jnp.float32
                )
                total = term if total is None else total + term
            if second == held and (first, second) not in ONE_WAY:
                term = lax.dot_general(
                    blocks[first][:depth], whole[r], (((1,), (0,)), ((), ())), preferred_element_type=jnp.float32
                )
                total = term if total is None else total + term
        out[...] = total.astype(out.dtype)


def call(kernel, ins, out_shape, scratch=()):
    return pl.pallas_call(
        kernel,
        out_shape=out_shape,
        in_specs=ins,
        out_specs=jax.tree.map(lambda _: VMEM, out_shape),
        scratch_shapes=list(scratch),
        compiler_params=pltpu.CompilerParams(vmem_limit_bytes=16 * 1024 * 1024),
    )


def body(b_factors, occ_energy, vir_energy):
    f32, bf16 = jnp.float32, jnp.bfloat16
    shape = jax.ShapeDtypeStruct
    columns = b_factors.T
    depth, width = columns.shape
    square = pltpu.VMEM((width, width), f32)

    packed = call(pack_kernel, [VMEM, SMEM], shape((depth + HALF, width), bf16))(columns, occ_energy)
    blocks = [packed] + [send_home(packed, -s) for s in HELD[1:]]

    row, strip = call(strip_kernel, [VMEM], [shape((8, width), f32), shape((CHIP, width), f32)], [square])(
        vir_energy[None, :]
    )

    def halves(pairs):
        return [shape((8 * pairs * HALF, width), f32), shape((8 * pairs * HALF, width), bf16)]

    early = call(functools.partial(early_kernel, depth), [VMEM] * 3, halves(EARLY), [square])(
        blocks[0], blocks[3], blocks[4]
    )
    keep, send = call(functools.partial(late_kernel, depth), [VMEM] * 7, halves(len(PAIRS)), [square])(*blocks, *early)
    one, two, three, four, own = call(
        core_sum_kernel, [VMEM] * 2,
        [shape((n * SIZE, width), t) for n, t in ((2, bf16), (2, f32), (2, bf16), (1, bf16), (1, f32))],
    )(keep, sibling(send))
    four = along_z(four, 2)
    three = along_z(three, 1)
    one = along_z(one, 1)
    two = along_z(call(relay_kernel, [VMEM] * 3, shape((2 * SIZE, width), bf16))(two, three, four), 2)
    partial = call(chip_sum_kernel, [VMEM] * 3, shape((2 * SIZE, width), f32))(own, one, two)

    amplitude = call(functools.partial(amplitude_kernel, depth), [VMEM] * 9, shape((2 * SIZE, width), bf16))(
        *blocks, partial, sibling(partial), row, strip
    )
    two = along_z(amplitude, 2)
    one = along_z(amplitude, 1)
    three = along_z(two, 1)
    four = along_z(two, 2)
    mine = [one, two, three, four]
    other = [sibling(piece) for piece in mine[:3]]

    parts = call(
        functools.partial(gamma_kernel, depth),
        [VMEM] * 13,
        [shape((depth, width), bf16)] * 4 + [shape((len(PAIRS), width, width), bf16)],
    )(*blocks, amplitude, *mine, *other)
    *parts, whole = parts
    own = call(functools.partial(own_kernel, depth), [VMEM] * 6, [shape((depth, width), f32)])(*blocks, whole)[0]

    back = [send_home(parts[k - 1], HELD[k]) for k in (4, 3, 2, 1)]
    for part in back:
        own = own + part.astype(f32)
    return own.T


def solution(mesh):
    placed = (P("occ", "aux"), P("occ"), P())
    return jax.shard_map(
        body, mesh=mesh, in_specs=placed, out_specs=P("occ", "aux"), check_vma=False
    )
```
